32 devices in a mesh: fsdp: 8 (over z, x), rep: 4 (over y, core).
Axes of the slice: x: 2, y: 2, z: 4, core: 2. Of those that a mesh axis runs over, the one named last changes fastest.
Arguments:
- gate_shards: bfloat16 [4, 7168, 2048], P(None, 'fsdp', 'rep'), may hold values from -6 to 6
- up_shards: bfloat16 [4, 7168, 2048], P(None, 'fsdp', 'rep'), may hold values from -6 to 6
- norm_gain: float32 [7168], P('fsdp'), may hold values from 0.1 to 1.9
- matching: int32 [8], replicated, may hold values from 0 to 7, each once
- replica_slots: int32 [4, 4], replicated, may hold values from 0 to 7, as said below
- replica_count: int32 [4], replicated, may hold values from 1 to 4, as said below
Outputs:
- joined: bfloat16 [8, 7168, 4096], P('fsdp')
The draws below stay inside these ranges and needn't reach their ends.
Inputs may be any that keep to these rules, and one draw needn't show every extreme that they name: `replica_slots`: every physical slot 0 to 7 appears exactly once among the first replica_count[e] entries of the rows e together; those entries of a row are ascending; the remaining entries of a row are arbitrary slots. `replica_count`: the counts sum to 8 and stay at or below 4; one expert has exactly 4 replicas in every draw. `matching`: each rank appears once.
All inputs are finite; a program needn't handle non-finite values.
Results may differ from the reference program's by a relative error of at most 0.001.
Values may be sent and summed in bfloat16 or wider, within the bound.
A program may use at most 256 MiB of HBM per device.

```python
import jax
import jax.numpy as jnp

D = 7168
FF = 2048
NB = 1
FFU = 2048
SLOTS = 8
E = 4
MAXREP = 4
N_FSDP = 8


def replica_tables(key):
    order = jax.random.permutation(jax.random.fold_in(key, 1), SLOTS)
    hottest = jax.random.randint(jax.random.fold_in(key, 2), (), 0, E)
    positions = jnp.arange(SLOTS, dtype=jnp.int32)
    spare = max(E - 1, 1)
    pick_other = jax.random.randint(jax.random.fold_in(key, 3), (SLOTS,), 0, spare)
    rotate = jax.random.permutation(jax.random.fold_in(key, 4), spare)
    others = (hottest + 1 + rotate[pick_other]) % E
    owner_at = jnp.where(positions < E, positions, jnp.where(positions < E + MAXREP - 1, hottest, others))
    slot_owners = jnp.zeros((SLOTS,), jnp.int32).at[order].set(owner_at.astype(jnp.int32))
    counts = jnp.sum((slot_owners[None, :] == jnp.arange(E)[:, None]).astype(jnp.int32), axis=1)
    listing = jnp.argsort(slot_owners * SLOTS + positions, stable=True).astype(jnp.int32)
    starts = jnp.cumsum(counts) - counts
    table = listing[jnp.clip(starts[:, None] + jnp.arange(MAXREP)[None, :], 0, SLOTS - 1)]
    return (table.astype(jnp.int32), counts.astype(jnp.int32))


def draw_replica_slots(key, part):
    table, counts = replica_tables(key)
    key = jax.random.fold_in(key, 7)
    filler = jax.random.randint(key, (E, MAXREP), 0, SLOTS)
    live = jnp.arange(MAXREP)[None, :] < counts[:, None]
    return jnp.where(live, table, filler).astype(jnp.int32)


def draw_replica_count(key, part):
    table, counts = replica_tables(key)
    return counts.astype(jnp.int32)


def shard_levels(rng, extent, cuts, low, largest):
    def one(dim, parts):
        draws = jax.random.uniform(jax.random.fold_in(jax.random.fold_in(rng, 6), dim), (parts,), jnp.float32, low / len(cuts), largest / len(cuts))
        return jnp.repeat(jnp.exp(draws), extent[dim] // parts).reshape((-1,) + (1,) * (len(extent) - dim - 1))

    level = one(*cuts[0])
    for cut in cuts[1:]:
        level = level * one(*cut)
    return level


def scatter_about(stream_key, shape, spread, most, cuts=(), kind=jnp.bfloat16):
    factor_of = shard_levels(stream_key, shape, cuts, -0.22, 0.18) if cuts else 1.0
    result = jax.random.normal(stream_key, shape, jnp.float32) * spread * factor_of
    return jnp.minimum(jnp.maximum(result, -most), most).astype(kind)


def setup_inputs(seed: int = 0) -> dict:
    key_of = jax.random.split(jax.random.key(seed), 7)
    gate_shards = scatter_about(key_of[0], (E, D, FF), 1.0, 6.0, ((1, 8), (2, 4)))
    up_shards = scatter_about(key_of[1], (E, D, FF), 1.0, 6.0, ((1, 8), (2, 4)))
    norm_gain = jnp.clip(1.0 + 0.18 * jax.random.normal(key_of[2], (D,), jnp.float32), 0.1, 1.9)
    matching = jax.random.permutation(key_of[3], N_FSDP).astype(jnp.int32)
    replica_slots = draw_replica_slots(jax.random.fold_in(key_of[6], 71), 0)
    replica_count = draw_replica_count(jax.random.fold_in(key_of[6], 71), 0)
    return dict(gate_shards=gate_shards, up_shards=up_shards, norm_gain=norm_gain, matching=matching, replica_slots=replica_slots, replica_count=replica_count)


def slot_owner(replica_slots, replica_count, slots):
    live = jnp.arange(replica_slots.shape[1])[None, :] < replica_count[:, None]
    hits = live[:, :, None] & (replica_slots[:, :, None] == jnp.arange(slots)[None, None, :])
    owners = jnp.arange(replica_slots.shape[0], dtype=jnp.int32)[:, None, None] * hits.astype(jnp.int32)
    return jnp.sum(owners, axis=(0, 1)).astype(jnp.int32)


def inverse_order(matching):
    count = matching.shape[0]
    match_grid = matching[None, :] == jnp.arange(count, dtype=jnp.int32)[:, None]
    ranks = jnp.where(match_grid, jnp.arange(count, dtype=jnp.int32)[None, :], 0)
    return jnp.sum(ranks, axis=1).astype(jnp.int32)


def reference(gate_shards, up_shards, norm_gain, matching, replica_slots, replica_count):
    rows = D // N_FSDP
    owners = slot_owner(replica_slots, replica_count, SLOTS)
    targets = jnp.arange(N_FSDP, dtype=jnp.int32)
    expert_pick = owners[targets // NB]
    block_pick = targets % NB
    inverse = inverse_order(matching)
    gate_model = gate_shards.reshape(E, N_FSDP, rows, FF)[:, inverse].reshape(E, D, FF)
    up_model = up_shards.reshape(E, N_FSDP, rows, FF)[:, inverse].reshape(E, D, FF)
    gain_model = norm_gain.reshape(N_FSDP, rows)[inverse].reshape(D)
    gate_pick = gate_model.reshape(E, D, FFU, NB)[expert_pick, :, :, block_pick]
    up_pick = up_model.reshape(E, D, FFU, NB)[expert_pick, :, :, block_pick]
    gate_fold = (gate_pick.astype(jnp.float32) * gain_model[None, :, None]).astype(jnp.bfloat16)
    up_fold = (up_pick.astype(jnp.float32) * gain_model[None, :, None]).astype(jnp.bfloat16)
    return jnp.stack((gate_fold, up_fold), axis=-1).reshape(N_FSDP, D, 2 * FFU)
```

```python
import functools

import jax
import jax.numpy as jnp
from jax import lax
from jax.experimental import pallas as pl
from jax.experimental.pallas import tpu as pltpu
from jax.sharding import PartitionSpec as P


def slot_owner(replica_slots, replica_count, slots):
    live = jnp.arange(replica_slots.shape[1])[None, :] < replica_count[:, None]
    hits = live[:, :, None] & (replica_slots[:, :, None] == jnp.arange(slots)[None, None, :])
    owners = jnp.arange(replica_slots.shape[0], dtype=jnp.int32)[:, None, None] * hits.astype(
        jnp.int32
    )
    return jnp.sum(owners, axis=(0, 1))


def inverse_order(matching):
    count = matching.shape[0]
    match_grid = matching[None, :] == jnp.arange(count, dtype=jnp.int32)[:, None]
    ranks = jnp.where(match_grid, jnp.arange(count, dtype=jnp.int32)[None, :], 0)
    return jnp.sum(ranks, axis=1)


def fold_rows(weights, gain_rows):
    return (weights.astype(jnp.float32) * gain_rows[:, None]).astype(jnp.bfloat16)


def pick_units(weights, expert_pick, block_pick, block_count):
    experts, rows, units = weights.shape
    return weights.reshape(experts, rows, units // block_count, block_count)[
        expert_pick, :, :, block_pick
    ]


def alternate(gate_part, up_part):
    shape = gate_part.shape
    return jnp.stack((gate_part, up_part), axis=-1).reshape(shape[:-1] + (2 * shape[-1],))


def local(gate_shards, up_shards, norm_gain, matching, replica_slots, replica_count):
    devices = lax.axis_size("fsdp")
    block_count = min(8, devices // 8)
    rows = gate_shards.shape[1]
    owners = slot_owner(replica_slots, replica_count, devices // block_count)
    targets = jnp.arange(devices, dtype=jnp.int32)
    expert_pick = owners[targets // block_count]
    block_pick = targets % block_count
    inverse = inverse_order(matching)
    gate_all, up_all = (
        lax.all_gather(gate_shards, "rep", axis=2, tiled=True),
        lax.all_gather(up_shards, "rep", axis=2, tiled=True),
    )
    outgoing = alternate(
        pick_units(gate_all, expert_pick, block_pick, block_count),
        pick_units(up_all, expert_pick, block_pick, block_count),
    )
    received = lax.all_to_all(outgoing, "fsdp", split_axis=0, concat_axis=0, tiled=True)
    portion = received[inverse].reshape(devices * rows, received.shape[2])
    gain_all = lax.all_gather(norm_gain, "fsdp", axis=0, tiled=True)
    gain_model = gain_all.reshape(devices, rows)[inverse].reshape(devices * rows)
    portion = fold_rows(portion, gain_model)
    return portion[None]


MESH = pl.DeviceIdType.MESH
LANES = 128
CHUNKS = 4


def fold_kernel(owners, gate_ref, up_ref, gain_ref, mix_ref, out_ref):
    gain = gain_ref[...]
    gate = (gate_ref[0].astype(jnp.float32) * gain).astype(jnp.bfloat16)
    up = (up_ref[0].astype(jnp.float32) * gain).astype(jnp.bfloat16)
    mix = mix_ref[...]
    for u in range(gate.shape[1] // LANES):
        both = jnp.concatenate(
            (gate[:, u * LANES : (u + 1) * LANES], up[:, u * LANES : (u + 1) * LANES]), axis=1
        )
        out_ref[0, :, 2 * u * LANES : 2 * (u + 1) * LANES] = jnp.dot(
            both, mix, preferred_element_type=jnp.float32
        ).astype(jnp.bfloat16)


def fold_slots(owners, gate, up, gain, slots):
    _, rows, units = gate.shape
    step = rows // 2
    k = jnp.arange(2 * LANES)
    mix = (k[None, :] == jnp.where(k < LANES, 2 * k, 2 * (k - LANES) + 1)[:, None]).astype(
        jnp.bfloat16
    )
    spec = pl.BlockSpec((1, step, units), lambda s, i, owners: (owners[s], i, 0))
    return pl.pallas_call(
        fold_kernel,
        out_shape=jax.ShapeDtypeStruct((slots, rows, 2 * units), jnp.bfloat16),
        grid_spec=pltpu.PrefetchScalarGridSpec(
            num_scalar_prefetch=1,
            grid=(slots, rows // step),
            in_specs=[
                spec,
                spec,
                pl.BlockSpec((step, 1), lambda s, i, owners: (i, 0)),
                pl.BlockSpec((2 * LANES, 2 * LANES), lambda s, i, owners: (0, 0)),
            ],
            out_specs=pl.BlockSpec((1, step, 2 * units), lambda s, i, owners: (s, i, 0)),
        ),
        compiler_params=pltpu.CompilerParams(vmem_limit_bytes=32 << 20),
        name="fold",
    )(owners, gate, up, gain[:, None], mix)


def exchange_kernel(
    n, chunks, mine, all_ref, s1s, s1r, ys, yr, c0s, c0r, c1s, c1r, own_sem
):
    f, r = lax.axis_index("fsdp"), lax.axis_index("rep")
    r_core = r + 1 - 2 * (r % 2)
    r_y = (r + 2) % 4
    _, rows, width = mine.shape
    size = rows // chunks

    barrier = pltpu.get_barrier_semaphore()
    for k in range(1, n):
        pl.semaphore_signal(barrier, inc=1, device_id=((f + k) % n, r), device_id_type=MESH)
    for other in (r_core, r_y):
        pl.semaphore_signal(barrier, inc=1, device_id=(f, other), device_id_type=MESH)
    pl.semaphore_wait(barrier, n + 1)

    def row(ch):
        return pl.ds(pl.multiple_of(ch * size, size), size)

    def region(i, ch, q):
        return all_ref.at[i, row(ch), pl.ds(pl.multiple_of(q * width, width), width)]

    def send(src, dst, device, send_sem, recv_sem, at):
        return pltpu.make_async_remote_copy(
            src_ref=src,
            dst_ref=dst,
            send_sem=send_sem.at[at],
            recv_sem=recv_sem.at[at],
            device_id=device,
            device_id_type=MESH,
        )

    def scatter(k, ch):
        d = (f + k) % n
        return send(mine.at[d, row(ch)], region(f, ch, r), (d, r), s1s, s1r, k * chunks + ch)

    def over_y(src, k, ch):
        return send(src, region((f + n - k) % n, ch, r), (f, r_y), ys, yr, k * chunks + ch)

    def over_core(src, k, ch):
        return send(src, region((f + n - k) % n, ch, r), (f, r_core), c0s, c0r, k * chunks + ch)

    def y_to_core(k, ch):
        part = region((f + n - k) % n, ch, r_y)
        return send(part, part, (f, r_core), c1s, c1r, k * chunks + ch)

    def held(k, ch):
        return region((f + n - k) % n, ch, r)

    def scatter_chunk(ch):
        def body(k, _):
            scatter(k, ch).start()
            return 0

        lax.fori_loop(1, n, body, 0)

    own = pltpu.make_async_copy(
        mine.at[f], all_ref.at[f, :, pl.ds(pl.multiple_of(r * width, width), width)], own_sem
    )
    scatter_chunk(0)

    def own_out(ch, _):
        over_y(mine.at[f, row(ch)], 0, ch).start()
        over_core(mine.at[f, row(ch)], 0, ch).start()
        return 0

    lax.fori_loop(0, chunks, own_out, 0)

    def later(ch, _):
        scatter_chunk(ch)
        return 0

    lax.fori_loop(1, chunks, later, 0)
    own.start()

    def pass_on(k, ch):
        over_y(held(k, ch), k, ch).wait_recv()
        y_to_core(k, ch).start()

    def step(t, _):
        k, ch = 1 + t % (n - 1), t // (n - 1)
        scatter(k, ch).wait_recv()
        over_y(held(k, ch), k, ch).start()
        over_core(held(k, ch), k, ch).start()

        @pl.when(t < chunks)
        def _():
            pass_on(0, t)

        @pl.when(t >= chunks)
        def _():
            u = t - chunks
            pass_on(1 + u % (n - 1), u // (n - 1))

        return 0

    lax.fori_loop(0, (n - 1) * chunks, step, 0)

    def last(t, _):
        u = (n - 1) * chunks - chunks + t
        pass_on(1 + u % (n - 1), u // (n - 1))
        return 0

    lax.fori_loop(0, chunks, last, 0)

    def finish(t, _):
        k, ch = t // chunks, t % chunks
        over_core(held(k, ch), k, ch).wait_recv()
        y_to_core(k, ch).wait_recv()
        over_y(held(k, ch), k, ch).wait_send()
        over_core(held(k, ch), k, ch).wait_send()
        y_to_core(k, ch).wait_send()
        return 0

    lax.fori_loop(0, n * chunks, finish, 0)

    def sent(t, _):
        scatter(1 + t // chunks, t % chunks).wait_send()
        return 0

    lax.fori_loop(0, (n - 1) * chunks, sent, 0)
    own.wait()


def exchange(mine, n, reps):
    _, rows, width = mine.shape
    count = n * CHUNKS
    return pl.pallas_call(
        functools.partial(exchange_kernel, n, CHUNKS),
        out_shape=jax.ShapeDtypeStruct((n, rows, reps * width), mine.dtype),
        in_specs=[pl.BlockSpec(memory_space=pl.ANY)],
        out_specs=pl.BlockSpec(memory_space=pl.ANY),
        scratch_shapes=[pltpu.SemaphoreType.DMA((count,))] * 8 + [pltpu.SemaphoreType.DMA],
        compiler_params=pltpu.CompilerParams(collective_id=0, has_side_effects=True),
        name="exchange",
    )(mine)


def place_kernel(matching, in_ref, out_ref):
    out_ref[...] = in_ref[0]


def place(matching, blocks):
    n, rows, width = blocks.shape
    cut = 2
    return pl.pallas_call(
        place_kernel,
        out_shape=jax.ShapeDtypeStruct((n * rows, width), blocks.dtype),
        grid_spec=pltpu.PrefetchScalarGridSpec(
            num_scalar_prefetch=1,
            grid=(n, cut),
            in_specs=[pl.BlockSpec((1, rows // cut, width), lambda i, j, matching: (i, j, 0))],
            out_specs=pl.BlockSpec(
                (rows // cut, width), lambda i, j, matching: (matching[i] * cut + j, 0)
            ),
        ),
        compiler_params=pltpu.CompilerParams(vmem_limit_bytes=40 << 20),
        name="place",
    )(matching, blocks)


def local_whole(gate_shards, up_shards, norm_gain, matching, replica_slots, replica_count):
    n, reps = lax.axis_size("fsdp"), lax.axis_size("rep")
    owners = slot_owner(replica_slots, replica_count, n)
    mine = fold_slots(owners, gate_shards, up_shards, norm_gain, n)
    return place(matching, exchange(mine, n, reps))[None]


def solution(mesh):
    whole_experts = mesh.shape["fsdp"] == 8 and mesh.shape["rep"] == 4
    return jax.shard_map(
        local_whole if whole_experts else local,
        mesh=mesh,
        in_specs=(P(None, "fsdp", "rep"), P(None, "fsdp", "rep"), P("fsdp"), P(), P(), P()),
        out_specs=P("fsdp", None, None),
        check_vma=False,
    )
```

```python
import functools

import jax
import jax.numpy as jnp
from jax import lax
from jax.experimental import pallas as pl
from jax.experimental.pallas import tpu as pltpu
from jax.sharding import PartitionSpec as P


def slot_owner(replica_slots, replica_count, slots):
    live = jnp.arange(replica_slots.shape[1])[None, :] < replica_count[:, None]
    hits = live[:, :, None] & (replica_slots[:, :, None] == jnp.arange(slots)[None, None, :])
    owners = jnp.arange(replica_slots.shape[0], dtype=jnp.int32)[:, None, None] * hits.astype(
        jnp.int32
    )
    return jnp.sum(owners, axis=(0, 1))


def inverse_order(matching):
    count = matching.shape[0]
    match_grid = matching[None, :] == jnp.arange(count, dtype=jnp.int32)[:, None]
    ranks = jnp.where(match_grid, jnp.arange(count, dtype=jnp.int32)[None, :], 0)
    return jnp.sum(ranks, axis=1)


def fold_rows(weights, gain_rows):
    return (weights.astype(jnp.float32) * gain_rows[:, None]).astype(jnp.bfloat16)


def pick_units(weights, expert_pick, block_pick, block_count):
    experts, rows, units = weights.shape
    return weights.reshape(experts, rows, units // block_count, block_count)[
        expert_pick, :, :, block_pick
    ]


def alternate(gate_part, up_part):
    shape = gate_part.shape
    return jnp.stack((gate_part, up_part), axis=-1).reshape(shape[:-1] + (2 * shape[-1],))


def local(gate_shards, up_shards, norm_gain, matching, replica_slots, replica_count):
    devices = lax.axis_size("fsdp")
    block_count = min(8, devices // 8)
    rows = gate_shards.shape[1]
    owners = slot_owner(replica_slots, replica_count, devices // block_count)
    targets = jnp.arange(devices, dtype=jnp.int32)
    expert_pick = owners[targets // block_count]
    block_pick = targets % block_count
    inverse = inverse_order(matching)
    gate_all, up_all = (
        lax.all_gather(gate_shards, "rep", axis=2, tiled=True),
        lax.all_gather(up_shards, "rep", axis=2, tiled=True),
    )
    outgoing = alternate(
        pick_units(gate_all, expert_pick, block_pick, block_count),
        pick_units(up_all, expert_pick, block_pick, block_count),
    )
    received = lax.all_to_all(outgoing, "fsdp", split_axis=0, concat_axis=0, tiled=True)
    portion = received[inverse].reshape(devices * rows, received.shape[2])
    gain_all = lax.all_gather(norm_gain, "fsdp", axis=0, tiled=True)
    gain_model = gain_all.reshape(devices, rows)[inverse].reshape(devices * rows)
    portion = fold_rows(portion, gain_model)
    return portion[None]


MESH = pl.DeviceIdType.MESH
LANES = 128
CHUNKS = 8
ROUNDS = 2


def fold_kernel(owners, gate_ref, up_ref, gain_ref, mix_ref, out_ref):
    gain = gain_ref[...]
    gate = (gate_ref[0].astype(jnp.float32) * gain).astype(jnp.bfloat16)
    up = (up_ref[0].astype(jnp.float32) * gain).astype(jnp.bfloat16)
    mix = mix_ref[...]
    for u in range(gate.shape[1] // LANES):
        both = jnp.concatenate(
            (gate[:, u * LANES : (u + 1) * LANES], up[:, u * LANES : (u + 1) * LANES]), axis=1
        )
        out_ref[0, :, 2 * u * LANES : 2 * (u + 1) * LANES] = jnp.dot(
            both, mix, preferred_element_type=jnp.float32
        ).astype(jnp.bfloat16)


def fold_slots(owners, gate, up, gain, slots):
    _, rows, units = gate.shape
    step = rows // 2
    k = jnp.arange(2 * LANES)
    mix = (k[None, :] == jnp.where(k < LANES, 2 * k, 2 * (k - LANES) + 1)[:, None]).astype(
        jnp.bfloat16
    )
    spec = pl.BlockSpec((1, step, units), lambda s, i, owners: (owners[s], i, 0))
    return pl.pallas_call(
        fold_kernel,
        out_shape=jax.ShapeDtypeStruct((slots, rows, 2 * units), jnp.bfloat16),
        grid_spec=pltpu.PrefetchScalarGridSpec(
            num_scalar_prefetch=1,
            grid=(slots, rows // step),
            in_specs=[
                spec,
                spec,
                pl.BlockSpec((step, 1), lambda s, i, owners: (i, 0)),
                pl.BlockSpec((2 * LANES, 2 * LANES), lambda s, i, owners: (0, 0)),
            ],
            out_specs=pl.BlockSpec((1, step, 2 * units), lambda s, i, owners: (s, i, 0)),
        ),
        compiler_params=pltpu.CompilerParams(vmem_limit_bytes=56 << 20),
        name="fold",
    )(owners, gate, up, gain[:, None], mix)


def exchange_kernel(
    n, chunks, mine, all_ref, s1s, s1r, ys, yr, c0s, c0r, c1s, c1r, own_sem
):
    f, r = lax.axis_index("fsdp"), lax.axis_index("rep")
    r_core = r + 1 - 2 * (r % 2)
    r_y = (r + 2) % 4
    _, rows, width = mine.shape
    size = rows // chunks

    barrier = pltpu.get_barrier_semaphore()
    for k in range(1, n):
        pl.semaphore_signal(barrier, inc=1, device_id=((f + k) % n, r), device_id_type=MESH)
    for other in (r_core, r_y):
        pl.semaphore_signal(barrier, inc=1, device_id=(f, other), device_id_type=MESH)
    pl.semaphore_wait(barrier, n + 1)

    def row(ch):
        return pl.ds(pl.multiple_of(ch * size, size), size)

    def region(i, ch, q):
        return all_ref.at[i, row(ch), pl.ds(pl.multiple_of(q * width, width), width)]

    def send(src, dst, device, send_sem, recv_sem, at):
        return pltpu.make_async_remote_copy(
            src_ref=src,
            dst_ref=dst,
            send_sem=send_sem.at[at],
            recv_sem=recv_sem.at[at],
            device_id=device,
            device_id_type=MESH,
        )

    def scatter(k, ch):
        d = (f + k) % n
        return send(mine.at[d, row(ch)], region(f, ch, r), (d, r), s1s, s1r, k * chunks + ch)

    def over_y(src, k, ch):
        return send(src, region((f + n - k) % n, ch, r), (f, r_y), ys, yr, k * chunks + ch)

    def over_core(src, k, ch):
        return send(src, region((f + n - k) % n, ch, r), (f, r_core), c0s, c0r, k * chunks + ch)

    def y_to_core(k, ch):
        part = region((f + n - k) % n, ch, r_y)
        return send(part, part, (f, r_core), c1s, c1r, k * chunks + ch)

    def held(k, ch):
        return region((f + n - k) % n, ch, r)

    window = ROUNDS * (n - 1)

    def scatter_at(t):
        return scatter(1 + t % (n - 1), t // (n - 1))

    def begin(t, _):
        scatter_at(t).start()
        return 0

    own = pltpu.make_async_copy(
        mine.at[f], all_ref.at[f, :, pl.ds(pl.multiple_of(r * width, width), width)], own_sem
    )
    lax.fori_loop(0, n - 1, begin, 0)

    def own_out(ch, _):
        over_y(mine.at[f, row(ch)], 0, ch).start()
        over_core(mine.at[f, row(ch)], 0, ch).start()
        return 0

    lax.fori_loop(0, chunks, own_out, 0)

    lax.fori_loop(n - 1, window, begin, 0)
    own.start()

    def pass_on(k, ch):
        over_y(held(k, ch), k, ch).wait_recv()
        y_to_core(k, ch).start()

    def step(t, _):
        k, ch = 1 + t % (n - 1), t // (n - 1)
        scatter(k, ch).wait_recv()
        over_y(held(k, ch), k, ch).start()
        over_core(held(k, ch), k, ch).start()
        scatter(k, ch).wait_send()

        @pl.when(t < (n - 1) * chunks - window)
        def _():
            scatter_at(t + window).start()

        @pl.when(t < chunks)
        def _():
            pass_on(0, t)

        @pl.when(t >= chunks)
        def _():
            u = t - chunks
            pass_on(1 + u % (n - 1), u // (n - 1))

        return 0

    lax.fori_loop(0, (n - 1) * chunks, step, 0)

    def last(t, _):
        u = (n - 1) * chunks - chunks + t
        pass_on(1 + u % (n - 1), u // (n - 1))
        return 0

    lax.fori_loop(0, chunks, last, 0)

    def finish(t, _):
        k, ch = t // chunks, t % chunks
        over_core(held(k, ch), k, ch).wait_recv()
        y_to_core(k, ch).wait_recv()
        over_y(held(k, ch), k, ch).wait_send()
        over_core(held(k, ch), k, ch).wait_send()
        y_to_core(k, ch).wait_send()
        return 0

    lax.fori_loop(0, n * chunks, finish, 0)

    own.wait()


def exchange(mine, n, reps):
    _, rows, width = mine.shape
    count = n * CHUNKS
    return pl.pallas_call(
        functools.partial(exchange_kernel, n, CHUNKS),
        out_shape=jax.ShapeDtypeStruct((n, rows, reps * width), mine.dtype),
        in_specs=[pl.BlockSpec(memory_space=pl.ANY)],
        out_specs=pl.BlockSpec(memory_space=pl.ANY),
        scratch_shapes=[pltpu.SemaphoreType.DMA((count,))] * 8 + [pltpu.SemaphoreType.DMA],
        compiler_params=pltpu.CompilerParams(collective_id=0, has_side_effects=True),
        name="exchange",
    )(mine)


def place_kernel(cut, matching, in_ref, out_ref, sems):
    n, rows, _ = in_ref.shape
    size = rows // cut

    def piece(i, j):
        return pltpu.make_async_copy(
            in_ref.at[i, pl.ds(j * size, size)],
            out_ref.at[pl.ds(pl.multiple_of(matching[i] * rows + j * size, size), size)],
            sems.at[i, j],
        )

    for i in range(n):
        for j in range(cut):
            piece(i, j).start()
    for i in range(n):
        for j in range(cut):
            piece(i, j).wait()


def place(matching, blocks):
    n, rows, width = blocks.shape
    cut = 4
    return pl.pallas_call(
        functools.partial(place_kernel, cut),
        out_shape=jax.ShapeDtypeStruct((n * rows, width), blocks.dtype),
        in_specs=[
            pl.BlockSpec(memory_space=pltpu.SMEM),
            pl.BlockSpec(memory_space=pl.ANY),
        ],
        out_specs=pl.BlockSpec(memory_space=pl.ANY),
        scratch_shapes=[pltpu.SemaphoreType.DMA((n, cut))],
        name="place",
    )(matching, blocks)


def local_whole(gate_shards, up_shards, norm_gain, matching, replica_slots, replica_count):
    n, reps = lax.axis_size("fsdp"), lax.axis_size("rep")
    owners = slot_owner(replica_slots, replica_count, n)
    mine = fold_slots(owners, gate_shards, up_shards, norm_gain, n)
    return place(matching, exchange(mine, n, reps))[None]


def solution(mesh):
    whole_experts = mesh.shape["fsdp"] == 8 and mesh.shape["rep"] == 4
    return jax.shard_map(
        local_whole if whole_experts else local,
        mesh=mesh,
        in_specs=(P(None, "fsdp", "rep"), P(None, "fsdp", "rep"), P("fsdp"), P(), P(), P()),
        out_specs=P("fsdp", None, None),
        check_vma=False,
    )
```

```python
import functools

import jax
import jax.numpy as jnp
from jax import lax
from jax.experimental import pallas as pl
from jax.experimental.pallas import tpu as pltpu
from jax.sharding import PartitionSpec as P


def slot_owner(replica_slots, replica_count, slots):
    live = jnp.arange(replica_slots.shape[1])[None, :] < replica_count[:, None]
    hits = live[:, :, None] & (replica_slots[:, :, None] == jnp.arange(slots)[None, None, :])
    owners = jnp.arange(replica_slots.shape[0], dtype=jnp.int32)[:, None, None] * hits.astype(
        jnp.int32
    )
    return jnp.sum(owners, axis=(0, 1))


def inverse_order(matching):
    count = matching.shape[0]
    match_grid = matching[None, :] == jnp.arange(count, dtype=jnp.int32)[:, None]
    ranks = jnp.where(match_grid, jnp.arange(count, dtype=jnp.int32)[None, :], 0)
    return jnp.sum(ranks, axis=1)


def fold_rows(weights, gain_rows):
    return (weights.astype(jnp.float32) * gain_rows[:, None]).astype(jnp.bfloat16)


def pick_units(weights, expert_pick, block_pick, block_count):
    experts, rows, units = weights.shape
    return weights.reshape(experts, rows, units // block_count, block_count)[
        expert_pick, :, :, block_pick
    ]


def alternate(gate_part, up_part):
    shape = gate_part.shape
    return jnp.stack((gate_part, up_part), axis=-1).reshape(shape[:-1] + (2 * shape[-1],))


def local(gate_shards, up_shards, norm_gain, matching, replica_slots, replica_count):
    devices = lax.axis_size("fsdp")
    block_count = min(8, devices // 8)
    rows = gate_shards.shape[1]
    owners = slot_owner(replica_slots, replica_count, devices // block_count)
    targets = jnp.arange(devices, dtype=jnp.int32)
    expert_pick = owners[targets // block_count]
    block_pick = targets % block_count
    inverse = inverse_order(matching)
    gate_all, up_all = (
        lax.all_gather(gate_shards, "rep", axis=2, tiled=True),
        lax.all_gather(up_shards, "rep", axis=2, tiled=True),
    )
    outgoing = alternate(
        pick_units(gate_all, expert_pick, block_pick, block_count),
        pick_units(up_all, expert_pick, block_pick, block_count),
    )
    received = lax.all_to_all(outgoing, "fsdp", split_axis=0, concat_axis=0, tiled=True)
    portion = received[inverse].reshape(devices * rows, received.shape[2])
    gain_all = lax.all_gather(norm_gain, "fsdp", axis=0, tiled=True)
    gain_model = gain_all.reshape(devices, rows)[inverse].reshape(devices * rows)
    portion = fold_rows(portion, gain_model)
    return portion[None]


MESH = pl.DeviceIdType.MESH
LANES = 128
CHUNKS = 8
ROUNDS = 2


def exchange_kernel(
    n,
    chunks,
    owners,
    gain_ref,
    gate_hbm,
    up_hbm,
    all_ref,
    gate,
    up,
    mix,
    mine,
    s1s,
    s1r,
    ys,
    yr,
    c0s,
    c0r,
    c1s,
    c1r,
    gate_sem,
    up_sem,
    own_sem,
):
    f, r = lax.axis_index("fsdp"), lax.axis_index("rep")
    r_core = r + 1 - 2 * (r % 2)
    r_y = (r + 2) % 4
    _, rows, width = mine.shape
    size = rows // chunks

    def row(ch):
        return pl.ds(pl.multiple_of(ch * size, size), size)

    def load(ch):
        return (
            pltpu.make_async_copy(gate_hbm.at[:, row(ch)], gate.at[:, row(ch)], gate_sem.at[ch]),
            pltpu.make_async_copy(up_hbm.at[:, row(ch)], up.at[:, row(ch)], up_sem.at[ch]),
        )

    def begin_load(ch, _):
        for copy in load(ch):
            copy.start()
        return 0

    lax.fori_loop(0, chunks, begin_load, 0)

    def mate(k):
        total, bit = 0, 1
        while bit < n:
            total = total + (f // bit + k // bit) % 2 * bit
            bit *= 2
        return total

    barrier = pltpu.get_barrier_semaphore()
    for k in range(1, n):
        pl.semaphore_signal(barrier, inc=1, device_id=(mate(k), r), device_id_type=MESH)
    for other in (r_core, r_y):
        pl.semaphore_signal(barrier, inc=1, device_id=(f, other), device_id_type=MESH)

    source = lax.broadcasted_iota(jnp.int32, mix.shape, 0)
    target = lax.broadcasted_iota(jnp.int32, mix.shape, 1)
    place_of = jnp.where(source < LANES, 2 * source, 2 * source - (2 * LANES - 1))
    mix[...] = jnp.where(place_of == target, 1.0, 0.0).astype(jnp.bfloat16)

    def fold(d, ch):
        e = owners[d]
        gain = gain_ref[row(ch), :]
        g = (gate[e, row(ch), :].astype(jnp.float32) * gain).astype(jnp.bfloat16)
        u = (up[e, row(ch), :].astype(jnp.float32) * gain).astype(jnp.bfloat16)
        for c in range(0, g.shape[1], LANES):
            both = jnp.concatenate((g[:, c : c + LANES], u[:, c : c + LANES]), axis=1)
            mine[d, row(ch), 2 * c : 2 * (c + LANES)] = jnp.dot(
                both, mix[...], preferred_element_type=jnp.float32
            ).astype(jnp.bfloat16)

    def region(i, ch, q):
        return all_ref.at[i, row(ch), pl.ds(pl.multiple_of(q * width, width), width)]

    def send(src, dst, device, send_sem, recv_sem, at):
        return pltpu.make_async_remote_copy(
            src_ref=src,
            dst_ref=dst,
            send_sem=send_sem.at[at],
            recv_sem=recv_sem.at[at],
            device_id=device,
            device_id_type=MESH,
        )

    def scatter(k, ch):
        d = mate(k)
        return send(mine.at[d, row(ch)], region(f, ch, r), (d, r), s1s, s1r, k * chunks + ch)

    def over_y(src, k, ch):
        return send(src, region(mate(k), ch, r), (f, r_y), ys, yr, k * chunks + ch)

    def over_core(src, k, ch):
        return send(src, region(mate(k), ch, r), (f, r_core), c0s, c0r, k * chunks + ch)

    def y_to_core(k, ch):
        part = region(mate(k), ch, r_y)
        return send(part, part, (f, r_core), c1s, c1r, k * chunks + ch)

    def held(k, ch):
        return region(mate(k), ch, r)

    window = ROUNDS * (n - 1)

    def at(t):
        p = t % (n - 1)
        return (p + 1) // 2 + (p + 1) % 2 * (n // 2), t // (n - 1)

    def begin(t, _):
        k, ch = at(t)
        fold(mate(k), ch)
        scatter(k, ch).start()
        return 0

    def loaded(ch, _):
        for copy in load(ch):
            copy.wait()
        return 0

    lax.fori_loop(0, chunks, loaded, 0)
    pl.semaphore_wait(barrier, n + 1)
    lax.fori_loop(0, n - 1, begin, 0)

    def own_out(ch, _):
        fold(f, ch)
        over_y(mine.at[f, row(ch)], 0, ch).start()
        over_core(mine.at[f, row(ch)], 0, ch).start()
        return 0

    lax.fori_loop(0, chunks, own_out, 0)
    lax.fori_loop(n - 1, window, begin, 0)
    own = pltpu.make_async_copy(
        mine.at[f], all_ref.at[f, :, pl.ds(pl.multiple_of(r * width, width), width)], own_sem
    )
    own.start()

    def pass_on(k, ch):
        over_y(held(k, ch), k, ch).wait_recv()
        y_to_core(k, ch).start()

    def step(t, _):
        k, ch = at(t)
        scatter(k, ch).wait_recv()
        over_y(held(k, ch), k, ch).start()
        over_core(held(k, ch), k, ch).start()
        scatter(k, ch).wait_send()

        @pl.when(t < (n - 1) * chunks - window)
        def _():
            begin(t + window, 0)

        @pl.when(t < chunks)
        def _():
            pass_on(0, t)

        @pl.when(t >= chunks)
        def _():
            pass_on(*at(t - chunks))

        return 0

    lax.fori_loop(0, (n - 1) * chunks, step, 0)

    def last(t, _):
        pass_on(*at(t))
        return 0

    lax.fori_loop((n - 2) * chunks, (n - 1) * chunks, last, 0)

    def finish(t, _):
        k, ch = t // chunks, t % chunks
        over_core(held(k, ch), k, ch).wait_recv()
        y_to_core(k, ch).wait_recv()
        over_y(held(k, ch), k, ch).wait_send()
        over_core(held(k, ch), k, ch).wait_send()
        y_to_core(k, ch).wait_send()
        return 0

    lax.fori_loop(0, n * chunks, finish, 0)
    own.wait()


def exchange(owners, gate, up, gain, n, reps):
    _, rows, units = gate.shape
    count = n * CHUNKS
    return pl.pallas_call(
        functools.partial(exchange_kernel, n, CHUNKS),
        out_shape=jax.ShapeDtypeStruct((n, rows, reps * 2 * units), gate.dtype),
        in_specs=[
            pl.BlockSpec(memory_space=pltpu.SMEM),
            pl.BlockSpec(memory_space=pltpu.VMEM),
            pl.BlockSpec(memory_space=pl.ANY),
            pl.BlockSpec(memory_space=pl.ANY),
        ],
        out_specs=pl.BlockSpec(memory_space=pl.ANY),
        scratch_shapes=[
            pltpu.VMEM(gate.shape, gate.dtype),
            pltpu.VMEM(up.shape, up.dtype),
            pltpu.VMEM((2 * LANES, 2 * LANES), gate.dtype),
            pltpu.VMEM((n, rows, 2 * units), gate.dtype),
        ]
        + [pltpu.SemaphoreType.DMA((count,))] * 8
        + [pltpu.SemaphoreType.DMA((CHUNKS,))] * 2
        + [pltpu.SemaphoreType.DMA],
        compiler_params=pltpu.CompilerParams(
            collective_id=0, has_side_effects=True, vmem_limit_bytes=56 << 20
        ),
        name="exchange",
    )(owners, gain[:, None], gate, up)


def place_kernel(cut, slots, matching, in_ref, out_ref, ring, in_sems, out_sems):
    n, rows, _ = in_ref.shape
    size = rows // cut
    pieces = n * cut

    def bring(p):
        return pltpu.make_async_copy(
            in_ref.at[p // cut, pl.ds(p % cut * size, size)],
            ring.at[p % slots],
            in_sems.at[p % slots],
        )

    def put(p):
        start = pl.multiple_of(matching[p // cut] * rows + p % cut * size, size)
        return pltpu.make_async_copy(
            ring.at[p % slots], out_ref.at[pl.ds(start, size)], out_sems.at[p % slots]
        )

    for p in range(slots):
        bring(p).start()
    for p in range(pieces):
        bring(p).wait()
        put(p).start()
        done = p - slots // 2
        if done >= 0 and done + slots < pieces:
            put(done).wait()
            bring(done + slots).start()
    for p in range(pieces - slots, pieces):
        put(p).wait()


def place(matching, blocks):
    n, rows, width = blocks.shape
    cut, slots = 4, 16
    return pl.pallas_call(
        functools.partial(place_kernel, cut, slots),
        out_shape=jax.ShapeDtypeStruct((n * rows, width), blocks.dtype),
        in_specs=[
            pl.BlockSpec(memory_space=pltpu.SMEM),
            pl.BlockSpec(memory_space=pl.ANY),
        ],
        out_specs=pl.BlockSpec(memory_space=pl.ANY),
        scratch_shapes=[
            pltpu.VMEM((slots, rows // cut, width), blocks.dtype),
            pltpu.SemaphoreType.DMA((slots,)),
            pltpu.SemaphoreType.DMA((slots,)),
        ],
        compiler_params=pltpu.CompilerParams(vmem_limit_bytes=40 << 20),
        name="place",
    )(matching, blocks)


def local_whole(gate_shards, up_shards, norm_gain, matching, replica_slots, replica_count):
    n, reps = lax.axis_size("fsdp"), lax.axis_size("rep")
    owners = slot_owner(replica_slots, replica_count, n)
    blocks = exchange(owners, gate_shards, up_shards, norm_gain, n, reps)
    return place(matching, blocks)[None]


def solution(mesh):
    whole_experts = mesh.shape["fsdp"] == 8 and mesh.shape["rep"] == 4
    return jax.shard_map(
        local_whole if whole_experts else local,
        mesh=mesh,
        in_specs=(P(None, "fsdp", "rep"), P(None, "fsdp", "rep"), P("fsdp"), P(), P(), P()),
        out_specs=P("fsdp", None, None),
        check_vma=False,
    )
```

```python
import functools

import jax
import jax.numpy as jnp
from jax import lax
from jax.experimental import pallas as pl
from jax.experimental.pallas import tpu as pltpu
from jax.sharding import PartitionSpec as P


def slot_owner(replica_slots, replica_count, slots):
    live = jnp.arange(replica_slots.shape[1])[None, :] < replica_count[:, None]
    hits = live[:, :, None] & (replica_slots[:, :, None] == jnp.arange(slots)[None, None, :])
    owners = jnp.arange(replica_slots.shape[0], dtype=jnp.int32)[:, None, None] * hits.astype(
        jnp.int32
    )
    return jnp.sum(owners, axis=(0, 1))


def inverse_order(matching):
    count = matching.shape[0]
    match_grid = matching[None, :] == jnp.arange(count, dtype=jnp.int32)[:, None]
    ranks = jnp.where(match_grid, jnp.arange(count, dtype=jnp.int32)[None, :], 0)
    return jnp.sum(ranks, axis=1)


def fold_rows(weights, gain_rows):
    return (weights.astype(jnp.float32) * gain_rows[:, None]).astype(jnp.bfloat16)


def pick_units(weights, expert_pick, block_pick, block_count):
    experts, rows, units = weights.shape
    return weights.reshape(experts, rows, units // block_count, block_count)[
        expert_pick, :, :, block_pick
    ]


def alternate(gate_part, up_part):
    shape = gate_part.shape
    return jnp.stack((gate_part, up_part), axis=-1).reshape(shape[:-1] + (2 * shape[-1],))


def local(gate_shards, up_shards, norm_gain, matching, replica_slots, replica_count):
    devices = lax.axis_size("fsdp")
    block_count = min(8, devices // 8)
    rows = gate_shards.shape[1]
    owners = slot_owner(replica_slots, replica_count, devices // block_count)
    targets = jnp.arange(devices, dtype=jnp.int32)
    expert_pick = owners[targets // block_count]
    block_pick = targets % block_count
    inverse = inverse_order(matching)
    gate_all, up_all = (
        lax.all_gather(gate_shards, "rep", axis=2, tiled=True),
        lax.all_gather(up_shards, "rep", axis=2, tiled=True),
    )
    outgoing = alternate(
        pick_units(gate_all, expert_pick, block_pick, block_count),
        pick_units(up_all, expert_pick, block_pick, block_count),
    )
    received = lax.all_to_all(outgoing, "fsdp", split_axis=0, concat_axis=0, tiled=True)
    portion = received[inverse].reshape(devices * rows, received.shape[2])
    gain_all = lax.all_gather(norm_gain, "fsdp", axis=0, tiled=True)
    gain_model = gain_all.reshape(devices, rows)[inverse].reshape(devices * rows)
    portion = fold_rows(portion, gain_model)
    return portion[None]


MESH = pl.DeviceIdType.MESH
LANES = 128
CHUNKS = 8
ROUNDS = 2


def exchange_kernel(
    n,
    chunks,
    owners,
    gain_ref,
    gate_hbm,
    up_hbm,
    all_ref,
    near_ref,
    gate,
    up,
    mix,
    mine,
    s1s,
    s1r,
    ys,
    yr,
    c0s,
    c0r,
    c1s,
    c1r,
    gate_sem,
    up_sem,
    own_sem,
):
    f, r = lax.axis_index("fsdp"), lax.axis_index("rep")
    r_core = r + 1 - 2 * (r % 2)
    r_y = (r + 2) % 4
    _, rows, width = mine.shape
    size = rows // chunks

    def row(ch):
        return pl.ds(pl.multiple_of(ch * size, size), size)

    def load(ch):
        return (
            pltpu.make_async_copy(gate_hbm.at[:, row(ch)], gate.at[:, row(ch)], gate_sem.at[ch]),
            pltpu.make_async_copy(up_hbm.at[:, row(ch)], up.at[:, row(ch)], up_sem.at[ch]),
        )

    def begin_load(ch, _):
        for copy in load(ch):
            copy.start()
        return 0

    lax.fori_loop(0, chunks, begin_load, 0)

    def mate(k):
        total, bit = 0, 1
        while bit < n:
            total = total + (f // bit + k // bit) % 2 * bit
            bit *= 2
        return total

    barrier = pltpu.get_barrier_semaphore()
    for k in range(1, n):
        pl.semaphore_signal(barrier, inc=1, device_id=(mate(k), r), device_id_type=MESH)
    for other in (r_core, r_y):
        pl.semaphore_signal(barrier, inc=1, device_id=(f, other), device_id_type=MESH)

    source = lax.broadcasted_iota(jnp.int32, mix.shape, 0)
    target = lax.broadcasted_iota(jnp.int32, mix.shape, 1)
    place_of = jnp.where(source < LANES, 2 * source, 2 * source - (2 * LANES - 1))
    mix[...] = jnp.where(place_of == target, 1.0, 0.0).astype(jnp.bfloat16)

    def fold(d, ch):
        e = owners[d]
        gain = gain_ref[row(ch), :]
        g = (gate[e, row(ch), :].astype(jnp.float32) * gain).astype(jnp.bfloat16)
        u = (up[e, row(ch), :].astype(jnp.float32) * gain).astype(jnp.bfloat16)
        for c in range(0, g.shape[1], LANES):
            both = jnp.concatenate((g[:, c : c + LANES], u[:, c : c + LANES]), axis=1)
            mine[d, row(ch), 2 * c : 2 * (c + LANES)] = jnp.dot(
                both, mix[...], preferred_element_type=jnp.float32
            ).astype(jnp.bfloat16)

    def region(i, ch, half):
        return all_ref.at[i, row(ch), pl.ds(half * width, width)]

    def send(src, dst, device, send_sem, recv_sem, at):
        return pltpu.make_async_remote_copy(
            src_ref=src,
            dst_ref=dst,
            send_sem=send_sem.at[at],
            recv_sem=recv_sem.at[at],
            device_id=device,
            device_id_type=MESH,
        )

    def scatter(k, ch):
        d = mate(k)
        return send(mine.at[d, row(ch)], region(f, ch, 0), (d, r), s1s, s1r, k * chunks + ch)

    def over_y(src, k, ch):
        return send(src, region(mate(k), ch, 1), (f, r_y), ys, yr, k * chunks + ch)

    def over_core(src, k, ch):
        part = near_ref.at[0, mate(k), row(ch)]
        return send(src, part, (f, r_core), c0s, c0r, k * chunks + ch)

    def y_to_core(k, ch):
        part = near_ref.at[1, mate(k), row(ch)]
        return send(region(mate(k), ch, 1), part, (f, r_core), c1s, c1r, k * chunks + ch)

    def held(k, ch):
        return region(mate(k), ch, 0)

    window = ROUNDS * (n - 1)

    def at(t):
        p = t % (n - 1)
        return (p + 1) // 2 + (p + 1) % 2 * (n // 2), t // (n - 1)

    def begin(t, _):
        k, ch = at(t)
        fold(mate(k), ch)
        scatter(k, ch).start()
        return 0

    def loaded(ch, _):
        for copy in load(ch):
            copy.wait()
        return 0

    lax.fori_loop(0, chunks, loaded, 0)
    pl.semaphore_wait(barrier, n + 1)
    lax.fori_loop(0, n - 1, begin, 0)

    def own_out(ch, _):
        fold(f, ch)
        over_y(mine.at[f, row(ch)], 0, ch).start()
        over_core(mine.at[f, row(ch)], 0, ch).start()
        return 0

    lax.fori_loop(0, chunks, own_out, 0)
    lax.fori_loop(n - 1, window, begin, 0)
    own = pltpu.make_async_copy(mine.at[f], all_ref.at[f, :, pl.ds(0, width)], own_sem)
    own.start()

    def pass_on(k, ch):
        over_y(held(k, ch), k, ch).wait_recv()
        y_to_core(k, ch).start()

    def step(t, _):
        k, ch = at(t)
        scatter(k, ch).wait_recv()
        over_y(held(k, ch), k, ch).start()
        over_core(held(k, ch), k, ch).start()
        scatter(k, ch).wait_send()

        @pl.when(t < (n - 1) * chunks - window)
        def _():
            begin(t + window, 0)

        @pl.when((t >= chunks) & (t < 2 * chunks))
        def _():
            pass_on(0, t - chunks)

        @pl.when(t >= 2 * chunks)
        def _():
            pass_on(*at(t - 2 * chunks))

        return 0

    lax.fori_loop(0, (n - 1) * chunks, step, 0)

    def last(t, _):
        pass_on(*at(t))
        return 0

    lax.fori_loop((n - 3) * chunks, (n - 1) * chunks, last, 0)

    def finish(t, _):
        k, ch = t // chunks, t % chunks
        over_core(held(k, ch), k, ch).wait_recv()
        y_to_core(k, ch).wait_recv()
        over_y(held(k, ch), k, ch).wait_send()
        over_core(held(k, ch), k, ch).wait_send()
        y_to_core(k, ch).wait_send()
        return 0

    lax.fori_loop(0, n * chunks, finish, 0)
    own.wait()


def exchange(owners, gate, up, gain, n, reps):
    _, rows, units = gate.shape
    count = n * CHUNKS
    return pl.pallas_call(
        functools.partial(exchange_kernel, n, CHUNKS),
        out_shape=(
            pltpu.HBM((n, rows, reps * units), gate.dtype),
            pltpu.VMEM((2, n, rows, 2 * units), gate.dtype),
        ),
        in_specs=[
            pl.BlockSpec(memory_space=pltpu.SMEM),
            pl.BlockSpec(memory_space=pltpu.VMEM),
            pl.BlockSpec(memory_space=pl.ANY),
            pl.BlockSpec(memory_space=pl.ANY),
        ],
        out_specs=(
            pl.BlockSpec(memory_space=pl.ANY),
            pl.BlockSpec(memory_space=pltpu.VMEM),
        ),
        scratch_shapes=[
            pltpu.VMEM(gate.shape, gate.dtype),
            pltpu.VMEM(up.shape, up.dtype),
            pltpu.VMEM((2 * LANES, 2 * LANES), gate.dtype),
            pltpu.VMEM((n, rows, 2 * units), gate.dtype),
        ]
        + [pltpu.SemaphoreType.DMA((count,))] * 8
        + [pltpu.SemaphoreType.DMA((CHUNKS,))] * 2
        + [pltpu.SemaphoreType.DMA],
        compiler_params=pltpu.CompilerParams(
            collective_id=0, has_side_effects=True, vmem_limit_bytes=26 << 20
        ),
        name="exchange",
    )(owners, gain[:, None], gate, up)


def place_kernel(
    cut, slots, matching, in_ref, near_ref, out_ref, ring, in_sems, out_sems, sems
):
    r = lax.axis_index("rep")
    r_core = r + 1 - 2 * (r % 2)
    _, n, rows, width = near_ref.shape
    size = rows // cut
    pieces = 2 * n * cut

    def target(i, start, count, q):
        first = pl.multiple_of(matching[i] * rows + start, count)
        return out_ref.at[
            pl.ds(first, count), pl.ds(pl.multiple_of(q * width, width), width)
        ]

    def split(p):
        return p // (2 * cut), p // 2 % cut * size, p % 2

    def bring(p):
        i, start, half = split(p)
        return pltpu.make_async_copy(
            in_ref.at[i, pl.ds(start, size), pl.ds(half * width, width)],
            ring.at[p % slots],
            in_sems.at[p % slots],
        )

    def put(p):
        i, start, half = split(p)
        return pltpu.make_async_copy(
            ring.at[p % slots],
            target(i, start, size, (r + 2 * half) % 4),
            out_sems.at[p % slots],
        )

    def whole(i, far):
        return pltpu.make_async_copy(
            near_ref.at[far, i], target(i, 0, rows, (r_core + 2 * far) % 4), sems.at[i, far]
        )

    for p in range(slots):
        bring(p).start()
    for p in range(pieces):
        if p % (2 * cut) == 0:
            for far in range(2):
                whole(p // (2 * cut), far).start()
        bring(p).wait()
        put(p).start()
        done = p - slots // 2
        if done >= 0 and done + slots < pieces:
            put(done).wait()
            bring(done + slots).start()
    for p in range(pieces - slots, pieces):
        put(p).wait()
    for i in range(n):
        for far in range(2):
            whole(i, far).wait()


def place(matching, blocks, near_blocks, reps):
    _, n, rows, width = near_blocks.shape
    cut, slots = 2, 16
    return pl.pallas_call(
        functools.partial(place_kernel, cut, slots),
        out_shape=jax.ShapeDtypeStruct((n * rows, reps * width), blocks.dtype),
        in_specs=[
            pl.BlockSpec(memory_space=pltpu.SMEM),
            pl.BlockSpec(memory_space=pltpu.HBM),
            pl.BlockSpec(memory_space=pl.ANY),
        ],
        out_specs=pl.BlockSpec(memory_space=pl.ANY),
        scratch_shapes=[
            pltpu.VMEM((slots, rows // cut, width), blocks.dtype),
            pltpu.SemaphoreType.DMA((slots,)),
            pltpu.SemaphoreType.DMA((slots,)),
            pltpu.SemaphoreType.DMA((n, 2)),
        ],
        compiler_params=pltpu.CompilerParams(vmem_limit_bytes=32 << 20),
        name="place",
    )(matching, blocks, near_blocks)


def local_whole(gate_shards, up_shards, norm_gain, matching, replica_slots, replica_count):
    n, reps = lax.axis_size("fsdp"), lax.axis_size("rep")
    owners = slot_owner(replica_slots, replica_count, n)
    parts = exchange(owners, gate_shards, up_shards, norm_gain, n, reps)
    near = pltpu.with_memory_space_constraint(parts[1], pltpu.VMEM)
    return place(matching, parts[0], near, reps)[None]


def solution(mesh):
    whole_experts = mesh.shape["fsdp"] == 8 and mesh.shape["rep"] == 4
    return jax.shard_map(
        local_whole if whole_experts else local,
        mesh=mesh,
        in_specs=(P(None, "fsdp", "rep"), P(None, "fsdp", "rep"), P("fsdp"), P(), P(), P()),
        out_specs=P("fsdp", None, None),
        check_vma=False,
    )
```
